32 devices in a mesh: layer: 2 (over x), row: 4 (over y, core), col: 4 (over z).
Axes of the slice: x: 2, y: 2, z: 4, core: 2. Of those that a mesh axis runs over, the one named last changes fastest.
Arguments:
- density: bfloat16 [3200, 3200], P('row', 'col'), may hold values from -2 to 2
- density_mask: int32 [32, 32], P('row', 'col'), may hold values 0 or 1
- square_mask: int32 [32, 32], P('row', 'col'), may hold values 0 or 1
- result_mask: int32 [32, 32], P('row', 'col'), may hold values 0 or 1
- block_perm: int32 [32], replicated, may hold values from 0 to 31, as said below
Outputs:
- purified: bfloat16 [3200, 3200], P('row', 'col')
The draws below stay inside these ranges and needn't reach their ends.
Inputs may be any that keep to these rules, and one draw needn't show every extreme that they name: `block_perm`: A permutation of the 32 block indices. For any two aligned groups of 8 indices, exactly 2 indices of the first group are mapped into the second group.
All inputs are finite; a program needn't handle non-finite values. No bound on the sum of `density_mask` or of `square_mask` or of `result_mask` on one device may be relied on, other than what follows from the above.
Results may differ from the reference program's by a relative error of at most 0.0049.
Values may be sent and summed in bfloat16 or wider, within the bound.
A program may use at most 64 MiB of HBM per device.

```python
import jax
import jax.numpy as jnp

TILE = 8
BLOCKS = 32
ORDER = 3200
SHARE = 2


def draw_density(key, part):
    scale = (ORDER * 0.5) ** (-1.0 / 3.0)
    first = jax.random.fold_in(key, 11)
    values = jax.random.truncated_normal(first, -4.0, 4.0, (ORDER, ORDER), jnp.float32)
    return (values * scale).astype(jnp.bfloat16)


def draw_block_perm(key, part):
    groups = BLOCKS // TILE
    local_keys = jax.random.split(jax.random.fold_in(key, 21), groups)
    place_keys = jax.random.split(jax.random.fold_in(key, 22), groups)
    local_perm = jax.vmap(lambda single: jax.random.permutation(single, TILE))(local_keys).astype(jnp.int32)
    place_perm = jax.vmap(lambda single: jax.random.permutation(single, TILE))(place_keys).astype(jnp.int32)
    source = jnp.arange(groups, dtype=jnp.int32)[:, None]
    target = local_perm // SHARE
    slot_index = source * SHARE + local_perm % SHARE
    position = target * TILE + place_perm[target, slot_index]
    return position.reshape(BLOCKS).astype(jnp.int32)


def touch_ends(values, rng, low, top_value):
    index_at = [jax.random.randint(jax.random.fold_in(rng, axis), (), 0, length) for axis, length in enumerate(values.shape)]
    widest = values.shape.index(max(values.shape))
    next_to = index_at[:widest] + [(index_at[widest] + 1) % values.shape[widest]] + index_at[widest + 1:]
    return values.at[tuple(index_at)].set(low).at[tuple(next_to)].set(top_value)


def setup_inputs(seed: int = 0) -> dict:
    streams_of = jax.random.split(jax.random.key(seed), 6)
    density = draw_density(jax.random.fold_in(streams_of[5], 71), 0)
    density_mask = touch_ends((jax.random.randint(streams_of[1], (BLOCKS, BLOCKS), 0, 2) < 1).astype(jnp.int32), jax.random.fold_in(streams_of[1], 1), 0, 1)
    square_mask = touch_ends((jax.random.randint(streams_of[2], (BLOCKS, BLOCKS), 0, 4) < 3).astype(jnp.int32), jax.random.fold_in(streams_of[2], 1), 0, 1)
    result_mask = touch_ends((jax.random.randint(streams_of[3], (BLOCKS, BLOCKS), 0, 4) < 3).astype(jnp.int32), jax.random.fold_in(streams_of[3], 1), 0, 1)
    block_perm = draw_block_perm(jax.random.fold_in(streams_of[5], 71), 0)
    return {"density": density, "density_mask": density_mask, "square_mask": square_mask, "result_mask": result_mask, "block_perm": block_perm}


def expand_mask(values, pattern):
    count = pattern.shape[0]
    width = values.shape[0] // count
    shaped = values.reshape(count, width, count, width)
    shaped = shaped * pattern[:, None, :, None].astype(values.dtype)
    return shaped.reshape(count * width, count * width)


def reorder_blocks(values, order):
    count = order.shape[0]
    width = values.shape[0] // count
    shaped = values.reshape(count, width, count, width)
    shaped = jnp.take(shaped, order, axis=0)
    shaped = jnp.take(shaped, order, axis=2)
    return shaped.reshape(count * width, count * width)


def reference(density, density_mask, square_mask, result_mask, block_perm):
    masked = expand_mask(density, density_mask)
    inverse = jnp.argsort(block_perm).astype(jnp.int32)
    grid = reorder_blocks(masked, inverse)
    square = expand_mask(jnp.dot(grid, grid, preferred_element_type=jnp.float32), square_mask).astype(jnp.bfloat16)
    cube = jnp.dot(square, grid, preferred_element_type=jnp.float32)
    result = expand_mask(3.0 * square.astype(jnp.float32) - 2.0 * cube, result_mask).astype(jnp.bfloat16)
    return reorder_blocks(result, block_perm.astype(jnp.int32))
```

```python
import functools

import jax
import jax.numpy as jnp
from jax import lax
from jax.experimental import pallas as pl
from jax.experimental.pallas import tpu as pltpu
from jax.sharding import PartitionSpec as P

MESH = pl.DeviceIdType.MESH
LANES = 128


def row_chunks(rows):
    first = (rows // 32 + 1) * 16
    return ((0, first), (first, rows - first))


def copy_to(src, dst, send_sem, recv_sem, device):
    return pltpu.make_async_remote_copy(
        src_ref=src,
        dst_ref=dst,
        send_sem=send_sem,
        recv_sem=recv_sem,
        device_id=device,
        device_id_type=MESH,
    )


class Line:
    def __init__(self, part, send, recv, pos, count, device):
        self.part, self.send, self.recv = part, send, recv
        self.pos, self.count, self.device = pos, count, device

    def copy(self, k, way):
        part = self.part(k)
        target = self.device(self.pos + (1, -1)[way])
        return copy_to(part, part, self.send.at[way, k], self.recv.at[k], target)

    def has(self, way):
        return (self.pos < self.count - 1, self.pos > 0)[way]

    def start(self, k, way):
        @pl.when(self.has(way))
        def _():
            self.copy(k, way).start()

    def start_own(self):
        self.start(self.pos, 0)
        self.start(self.pos, 1)

    def step(self, s, then=None):
        for way in (0, 1):
            k = self.pos + (-s, s)[way]

            @pl.when(jnp.logical_and(k >= 0, k < self.count))
            def _():
                self.copy(k, 1 - way).wait_recv()
                self.start(k, way)
                if then is not None:
                    then(k)

    def wait_sends(self):
        for k in range(self.count):
            for way in (0, 1):
                held = (k <= self.pos, k >= self.pos)[way]

                @pl.when(jnp.logical_and(held, self.has(way)))
                def _():
                    self.copy(k, way).wait_send()


def spread(size, width, blocks, along):
    shape = (size, blocks) if along == 0 else (blocks, size)
    element = lax.broadcasted_iota(jnp.int32, shape, along)
    block = lax.broadcasted_iota(jnp.int32, shape, 1 - along)
    inside = jnp.logical_and(element >= block * width, element < (block + 1) * width)
    return inside.astype(jnp.float32)


def dot(a, b):
    return jnp.dot(a, b, preferred_element_type=jnp.float32)


def kernel(n, layers, dens, dmask, smask, rmask, perm, out, B, A, S, acc, keep_s, keep_r, G,
           m_send, m_recv, g_send, g_recv, b_send, b_recv, t_send, t_recv,
           a_send, a_recv, s_send, s_recv, x_send, x_recv):
    l = lax.axis_index("layer")
    r = lax.axis_index("row")
    c = lax.axis_index("col")
    size = dens.shape[0]
    blocks = dmask.shape[0]
    width = size // blocks
    half = size // layers
    half_blocks = blocks // layers
    chunks = row_chunks(half)
    y, core = r // 2, r % 2
    ny = n // 2
    twin = {"row": y * 2 + 1 - core}
    other = {"layer": 1 - l}

    barrier = pltpu.get_barrier_semaphore()
    for step in range(1, n):
        pl.semaphore_signal(barrier, 1, device_id={"row": (r + step) % n}, device_id_type=MESH)
    pl.semaphore_signal(barrier, 1, device_id=other, device_id_type=MESH)

    @pl.when(c > 0)
    def _():
        pl.semaphore_signal(barrier, 1, device_id={"col": c - 1}, device_id_type=MESH)

    @pl.when(c < n - 1)
    def _():
        pl.semaphore_signal(barrier, 1, device_id={"col": c + 1}, device_id_type=MESH)

    lane = lax.broadcasted_iota(jnp.int32, (blocks, LANES), 1)
    line_no = lax.broadcasted_iota(jnp.int32, (blocks, LANES), 0)
    put_s = (lane == c * blocks + line_no).astype(jnp.float32)
    put_r = (lane == LANES // 2 + c * blocks + line_no).astype(jnp.float32)
    mine = pl.ds(pl.multiple_of(r * blocks, 8), blocks)
    G[c, mine, :] = dot(smask[...].astype(jnp.float32), put_s) + dot(rmask[...].astype(jnp.float32), put_r)

    rows_of = dot(spread(size, width, blocks, 0), dmask[...].astype(jnp.float32))
    keep = dot(rows_of, spread(size, width, blocks, 1))
    masked = jnp.where(keep > 0.5, dens[...], jnp.zeros_like(dens[...]))
    B[r] = masked
    top = pl.ds(pl.multiple_of(l * half, 16), half)
    A[c] = B[r, top, :]

    ends = jnp.where(c == 0, 1, 0) + jnp.where(c == n - 1, 1, 0)
    pl.semaphore_wait(barrier, n + 2 - ends)

    def mask_copy(step):
        place = G.at[c, mine]
        return copy_to(place, place, m_send.at[step], m_recv.at[step], {"row": (r + step) % n})

    for step in range(1, n):
        mask_copy(step).start()

    def at_col(k):
        return {"col": k}

    a_lines, s_lines = [], []
    for j, (off, rows) in enumerate(chunks):
        a_lines.append(Line(lambda k, off=off, rows=rows: A.at[k, pl.ds(off, rows)],
                            a_send.at[j], a_recv.at[j], c, n, at_col))
        s_lines.append(Line(lambda k, off=off, rows=rows: S.at[k, pl.ds(off, rows)],
                            s_send.at[j], s_recv.at[j], c, n, at_col))
    g_line = Line(lambda k: G.at[k], g_send, g_recv, c, n, at_col)
    b_line = Line(lambda k: B.at[k * 2 + core], b_send, b_recv, y, ny, lambda k: {"row": k * 2 + core})

    def twin_copy(k):
        place = B.at[k * 2 + core]
        return copy_to(place, place, t_send.at[k], t_recv.at[k], twin)

    for line in a_lines:
        line.start_own()
    b_line.start_own()
    twin_copy(y).start()

    for step in range(1, n):
        mask_copy(step).wait_recv()
    g_line.start_own()
    for line in a_lines:
        line.step(1)
    g_line.step(1)
    for s in range(1, ny):
        b_line.step(s, lambda k: twin_copy(k).start())
    for s in range(2, n):
        g_line.step(s)
        for line in a_lines if s < n - 1 else ():
            line.step(s)
    for k in range(ny):
        place = B.at[k * 2 + 1 - core]
        copy_to(place, place, t_send.at[k], t_recv.at[k], twin).wait_recv()

    whole = G[0]
    for k in range(1, n):
        whole = whole + G[k]
    row_at = lax.broadcasted_iota(jnp.int32, (half, n * blocks), 0)
    row_to = jnp.zeros((half, n * blocks), jnp.int32)
    for t in range(half_blocks):
        row_to = jnp.where(row_at >= t * width, perm[r * blocks + l * half_blocks + t], row_to)
    pick_rows = (row_to == lax.broadcasted_iota(jnp.int32, (half, n * blocks), 1)).astype(jnp.float32)
    picked = dot(pick_rows, whole)
    col_at = lax.broadcasted_iota(jnp.int32, (LANES, size), 1)
    col_to = jnp.zeros((LANES, size), jnp.int32)
    for t in range(blocks):
        col_to = jnp.where(col_at >= t * width, perm[c * blocks + t], col_to)
    slot = lax.broadcasted_iota(jnp.int32, (LANES, size), 0)
    keep_s[...] = dot(picked, (col_to == slot).astype(jnp.float32))
    keep_r[...] = dot(picked, (col_to + LANES // 2 == slot).astype(jnp.float32))

    def product(left, off, rows):
        acc[0:rows, :] = jnp.zeros((rows, size), jnp.float32)

        def body(k, carry):
            acc[0:rows, :] += dot(left[k, off:off + rows, :], B[k])
            return carry

        lax.fori_loop(0, n, body, 0)

    for j, (off, rows) in enumerate(chunks):
        a_lines[j].step(n - 1)
        product(A, off, rows)
        value = jnp.where(keep_s[off:off + rows, :] > 0.5, acc[0:rows, :], 0.0)
        S[c, off:off + rows, :] = value.astype(jnp.bfloat16)
        s_lines[j].start_own()

    def result_copy(j):
        off, rows = chunks[j]
        place = out.at[pl.ds(pl.multiple_of(l * half + off, 16), rows)]
        return copy_to(place, place, x_send.at[j], x_recv.at[j], other)

    for s in range(1, n - 1):
        for line in s_lines:
            line.step(s)
    for j, (off, rows) in enumerate(chunks):
        s_lines[j].step(n - 1)
        product(S, off, rows)
        value = 3.0 * S[c, off:off + rows, :].astype(jnp.float32) - 2.0 * acc[0:rows, :]
        value = jnp.where(keep_r[off:off + rows, :] > 0.5, value, 0.0)
        out[pl.ds(pl.multiple_of(l * half + off, 16), rows), :] = value.astype(jnp.bfloat16)
        result_copy(j).start()

    for j, (off, rows) in enumerate(chunks):
        place = out.at[pl.ds(pl.multiple_of((1 - l) * half + off, 16), rows)]
        copy_to(place, place, x_send.at[j], x_recv.at[j], other).wait_recv()
        result_copy(j).wait_send()
    for line in (g_line, b_line, *a_lines, *s_lines):
        line.wait_sends()
    for k in range(ny):
        twin_copy(k).wait_send()
    for step in range(1, n):
        mask_copy(step).wait_send()


def per_device(n, layers, density, density_mask, square_mask, result_mask, block_perm):
    size = density.shape[0]
    half = size // layers
    blocks = density_mask.shape[0]
    pieces = row_chunks(half)
    count = len(pieces)
    most = max(rows for _, rows in pieces)
    bf16, f32 = jnp.bfloat16, jnp.float32
    dma = pltpu.SemaphoreType.DMA
    vmem = pl.BlockSpec(memory_space=pltpu.VMEM)
    return pl.pallas_call(
        functools.partial(kernel, n, layers),
        out_shape=jax.ShapeDtypeStruct((size, size), bf16),
        in_specs=[vmem] * 4 + [pl.BlockSpec(memory_space=pltpu.SMEM)],
        out_specs=vmem,
        scratch_shapes=[
            pltpu.VMEM((n, size, size), bf16),
            pltpu.VMEM((n, half, size), bf16),
            pltpu.VMEM((n, half, size), bf16),
            pltpu.VMEM((most, size), f32),
            pltpu.VMEM((half, size), f32),
            pltpu.VMEM((half, size), f32),
            pltpu.VMEM((n, n * blocks, LANES), f32),
            dma((n,)), dma((n,)),
            dma((2, n)), dma((n,)),
            dma((2, n // 2)), dma((n // 2,)),
            dma((n // 2,)), dma((n // 2,)),
            dma((count, 2, n)), dma((count, n)),
            dma((count, 2, n)), dma((count, n)),
            dma((count,)), dma((count,)),
        ],
        compiler_params=pltpu.CompilerParams(
            collective_id=0, has_side_effects=True, vmem_limit_bytes=56 * 2**20
        ),
        cost_estimate=pl.CostEstimate(
            flops=4 * n * half * size * size, bytes_accessed=4 * size * size, transcendentals=0
        ),
    )(density, density_mask, square_mask, result_mask, block_perm)


def solution(mesh):
    in_specs = (P("row", "col"), P("row", "col"), P("row", "col"), P("row", "col"), P())
    return jax.shard_map(
        functools.partial(per_device, mesh.shape["row"], mesh.shape["layer"]),
        mesh=mesh,
        in_specs=in_specs,
        out_specs=P("row", "col"),
        check_vma=False,
    )
```

```python
import functools

import jax
import jax.numpy as jnp
from jax import lax
from jax.experimental import pallas as pl
from jax.experimental.pallas import tpu as pltpu
from jax.sharding import PartitionSpec as P

MESH = pl.DeviceIdType.MESH
LANES = 128


CHUNKS = 3


def row_chunks(rows):
    groups = rows // 16
    sizes = [16 * (groups // CHUNKS + (j < groups % CHUNKS)) for j in range(CHUNKS)]
    return tuple((sum(sizes[:j]), sizes[j]) for j in range(CHUNKS))


def tail_groups(rows, tail):
    per = LANES // tail
    high = -(-rows // (16 * per)) * 16
    assert rows % high == 0
    return high, rows // high


def copy_to(src, dst, send_sem, recv_sem, device):
    return pltpu.make_async_remote_copy(
        src_ref=src,
        dst_ref=dst,
        send_sem=send_sem,
        recv_sem=recv_sem,
        device_id=device,
        device_id_type=MESH,
    )


class Line:
    def __init__(self, part, send, recv, pos, count, device):
        self.part, self.send, self.recv = part, send, recv
        self.pos, self.count, self.device = pos, count, device

    def copy(self, k, way):
        part = self.part(k)
        target = self.device(self.pos + (1, -1)[way])
        return copy_to(part, part, self.send.at[way, k], self.recv.at[k], target)

    def has(self, way):
        return (self.pos < self.count - 1, self.pos > 0)[way]

    def start(self, k, way):
        @pl.when(self.has(way))
        def _():
            self.copy(k, way).start()

    def start_own(self):
        self.start(self.pos, 0)
        self.start(self.pos, 1)

    def step(self, s, then=None):
        for way in (0, 1):
            k = self.pos + (-s, s)[way]

            @pl.when(jnp.logical_and(k >= 0, k < self.count))
            def _():
                self.copy(k, 1 - way).wait_recv()
                self.start(k, way)
                if then is not None:
                    then(k)

    def wait_sends(self):
        for k in range(self.count):
            for way in (0, 1):
                held = (k <= self.pos, k >= self.pos)[way]

                @pl.when(jnp.logical_and(held, self.has(way)))
                def _():
                    self.copy(k, way).wait_send()


def spread(size, width, blocks, along):
    shape = (size, blocks) if along == 0 else (blocks, size)
    element = lax.broadcasted_iota(jnp.int32, shape, along)
    block = lax.broadcasted_iota(jnp.int32, shape, 1 - along)
    inside = jnp.logical_and(element >= block * width, element < (block + 1) * width)
    return inside.astype(jnp.float32)


def dot(a, b):
    return jnp.dot(a, b, preferred_element_type=jnp.float32)


def shift(tail, g, wide):
    shape = (tail, LANES) if wide else (LANES, tail)
    narrow = lax.broadcasted_iota(jnp.int32, shape, 1 - wide)
    lane = lax.broadcasted_iota(jnp.int32, shape, int(wide))
    return (lane == g * tail + narrow).astype(jnp.bfloat16)


def pack(src, k, off, rows, dst, j, main, tail):
    high, count = tail_groups(rows, tail)
    total = jnp.zeros((high, LANES), jnp.float32)
    for g in range(count):
        at = off + g * high
        total = total + dot(src[k, at:at + high, main:main + tail], shift(tail, g, True))
    dst[k, j, 0:high, :] = total.astype(jnp.bfloat16)


def unpack(src, k, j, off, rows, dst, main, tail):
    high, count = tail_groups(rows, tail)
    packed = src[k, j, 0:high, :]
    for g in range(count):
        at = off + g * high
        dst[k, at:at + high, main:main + tail] = dot(packed, shift(tail, g, False)).astype(jnp.bfloat16)


def kernel(n, layers, dens, dmask, smask, rmask, perm, out, B, A, S, AT, ST, acc, keep_s, keep_r, G,
           m_send, m_recv, g_send, g_recv, b_send, b_recv, t_send, t_recv,
           a_send, a_recv, s_send, s_recv, at_send, at_recv, st_send, st_recv, x_send, x_recv):
    l = lax.axis_index("layer")
    r = lax.axis_index("row")
    c = lax.axis_index("col")
    size = dens.shape[0]
    blocks = dmask.shape[0]
    width = size // blocks
    half = size // layers
    half_blocks = blocks // layers
    chunks = row_chunks(half)
    tail = size % LANES
    main = size - tail
    y, core = r // 2, r % 2
    ny = n // 2
    twin = {"row": y * 2 + 1 - core}
    other = {"layer": 1 - l}

    barrier = pltpu.get_barrier_semaphore()
    for step in range(1, n):
        pl.semaphore_signal(barrier, 1, device_id={"row": (r + step) % n}, device_id_type=MESH)
    pl.semaphore_signal(barrier, 1, device_id=other, device_id_type=MESH)

    @pl.when(c > 0)
    def _():
        pl.semaphore_signal(barrier, 1, device_id={"col": c - 1}, device_id_type=MESH)

    @pl.when(c < n - 1)
    def _():
        pl.semaphore_signal(barrier, 1, device_id={"col": c + 1}, device_id_type=MESH)

    lane = lax.broadcasted_iota(jnp.int32, (blocks, LANES), 1)
    line_no = lax.broadcasted_iota(jnp.int32, (blocks, LANES), 0)
    put_s = (lane == c * blocks + line_no).astype(jnp.float32)
    put_r = (lane == LANES // 2 + c * blocks + line_no).astype(jnp.float32)
    mine = pl.ds(pl.multiple_of(r * blocks, 8), blocks)
    G[c, mine, :] = dot(smask[...].astype(jnp.float32), put_s) + dot(rmask[...].astype(jnp.float32), put_r)

    rows_of = dot(spread(size, width, blocks, 0), dmask[...].astype(jnp.float32))
    keep = dot(rows_of, spread(size, width, blocks, 1))
    masked = jnp.where(keep > 0.5, dens[...], jnp.zeros_like(dens[...]))
    B[r] = masked
    top = pl.ds(pl.multiple_of(l * half, 16), half)
    A[c] = B[r, top, :]
    for j, (off, rows) in enumerate(chunks):
        pack(A, c, off, rows, AT, j, main, tail)

    ends = jnp.where(c == 0, 1, 0) + jnp.where(c == n - 1, 1, 0)
    pl.semaphore_wait(barrier, n + 2 - ends)

    def mask_copy(step):
        place = G.at[c, mine]
        return copy_to(place, place, m_send.at[step], m_recv.at[step], {"row": (r + step) % n})

    for step in range(1, n):
        mask_copy(step).start()

    def at_col(k):
        return {"col": k}

    def lines_of(whole_part, tail_part, send, recv, tail_send, tail_recv):
        made = []
        for j, (off, rows) in enumerate(chunks):
            high, _ = tail_groups(rows, tail)
            made.append((
                Line(lambda k, j=j, high=high: tail_part.at[k, j, pl.ds(0, high)],
                     tail_send.at[j], tail_recv.at[j], c, n, at_col),
                Line(lambda k, off=off, rows=rows: whole_part.at[k, pl.ds(off, rows), pl.ds(0, main)],
                     send.at[j], recv.at[j], c, n, at_col),
            ))
        return made

    a_lines = lines_of(A, AT, a_send, a_recv, at_send, at_recv)
    s_lines = lines_of(S, ST, s_send, s_recv, st_send, st_recv)

    def start_own(pair):
        for line in pair:
            line.start_own()

    def step_all(pair, s):
        for line in pair:
            line.step(s)

    g_line = Line(lambda k: G.at[k], g_send, g_recv, c, n, at_col)
    b_line = Line(lambda k: B.at[k * 2 + core], b_send, b_recv, y, ny, lambda k: {"row": k * 2 + core})

    def twin_copy(k):
        place = B.at[k * 2 + core]
        return copy_to(place, place, t_send.at[k], t_recv.at[k], twin)

    for pair in a_lines:
        start_own(pair)
    b_line.start_own()
    twin_copy(y).start()

    for step in range(1, n):
        mask_copy(step).wait_recv()
    g_line.start_own()
    for pair in a_lines:
        step_all(pair, 1)
    g_line.step(1)
    for s in range(1, ny):
        b_line.step(s, lambda k: twin_copy(k).start())
    for s in range(2, n):
        g_line.step(s)
        for pair in a_lines if s < n - 1 else ():
            step_all(pair, s)
    for k in range(ny):
        place = B.at[k * 2 + 1 - core]
        copy_to(place, place, t_send.at[k], t_recv.at[k], twin).wait_recv()

    whole = G[0]
    for k in range(1, n):
        whole = whole + G[k]
    row_at = lax.broadcasted_iota(jnp.int32, (half, n * blocks), 0)
    row_to = jnp.zeros((half, n * blocks), jnp.int32)
    for t in range(half_blocks):
        row_to = jnp.where(row_at >= t * width, perm[r * blocks + l * half_blocks + t], row_to)
    pick_rows = (row_to == lax.broadcasted_iota(jnp.int32, (half, n * blocks), 1)).astype(jnp.float32)
    picked = dot(pick_rows, whole)
    col_at = lax.broadcasted_iota(jnp.int32, (LANES, size), 1)
    col_to = jnp.zeros((LANES, size), jnp.int32)
    for t in range(blocks):
        col_to = jnp.where(col_at >= t * width, perm[c * blocks + t], col_to)
    slot = lax.broadcasted_iota(jnp.int32, (LANES, size), 0)
    keep_s[...] = dot(picked, (col_to == slot).astype(jnp.float32))
    keep_r[...] = dot(picked, (col_to + LANES // 2 == slot).astype(jnp.float32))

    def product(left, tails, j, off, rows):
        acc[0:rows, :] = jnp.zeros((rows, size), jnp.float32)

        def body(k, carry):
            @pl.when(k != c)
            def _():
                unpack(tails, k, j, off, rows, left, main, tail)

            acc[0:rows, :] += dot(left[k, off:off + rows, :], B[k])
            return carry

        lax.fori_loop(0, n, body, 0)

    for j, (off, rows) in enumerate(chunks):
        step_all(a_lines[j], n - 1)
        product(A, AT, j, off, rows)
        value = jnp.where(keep_s[off:off + rows, :] > 0.5, acc[0:rows, :], 0.0)
        S[c, off:off + rows, :] = value.astype(jnp.bfloat16)
        pack(S, c, off, rows, ST, j, main, tail)
        start_own(s_lines[j])

    def result_copy(j):
        off, rows = chunks[j]
        place = out.at[pl.ds(pl.multiple_of(l * half + off, 16), rows)]
        return copy_to(place, place, x_send.at[j], x_recv.at[j], other)

    for s in range(1, n - 1):
        for pair in s_lines:
            step_all(pair, s)
    for j, (off, rows) in enumerate(chunks):
        step_all(s_lines[j], n - 1)
        product(S, ST, j, off, rows)
        value = 3.0 * S[c, off:off + rows, :].astype(jnp.float32) - 2.0 * acc[0:rows, :]
        value = jnp.where(keep_r[off:off + rows, :] > 0.5, value, 0.0)
        out[pl.ds(pl.multiple_of(l * half + off, 16), rows), :] = value.astype(jnp.bfloat16)
        result_copy(j).start()

    for j, (off, rows) in enumerate(chunks):
        place = out.at[pl.ds(pl.multiple_of((1 - l) * half + off, 16), rows)]
        copy_to(place, place, x_send.at[j], x_recv.at[j], other).wait_recv()
        result_copy(j).wait_send()
    for line in (g_line, b_line, *(line for pair in (*a_lines, *s_lines) for line in pair)):
        line.wait_sends()
    for k in range(ny):
        twin_copy(k).wait_send()
    for step in range(1, n):
        mask_copy(step).wait_send()


def per_device(n, layers, density, density_mask, square_mask, result_mask, block_perm):
    size = density.shape[0]
    half = size // layers
    blocks = density_mask.shape[0]
    pieces = row_chunks(half)
    count = len(pieces)
    most = max(rows for _, rows in pieces)
    high = max(tail_groups(rows, size % LANES)[0] for _, rows in pieces)
    bf16, f32 = jnp.bfloat16, jnp.float32
    dma = pltpu.SemaphoreType.DMA
    vmem = pl.BlockSpec(memory_space=pltpu.VMEM)
    return pl.pallas_call(
        functools.partial(kernel, n, layers),
        out_shape=jax.ShapeDtypeStruct((size, size), bf16),
        in_specs=[vmem] * 4 + [pl.BlockSpec(memory_space=pltpu.SMEM)],
        out_specs=vmem,
        scratch_shapes=[
            pltpu.VMEM((n, size, size), bf16),
            pltpu.VMEM((n, half, size), bf16),
            pltpu.VMEM((n, half, size), bf16),
            pltpu.VMEM((n, count, high, LANES), bf16),
            pltpu.VMEM((n, count, high, LANES), bf16),
            pltpu.VMEM((most, size), f32),
            pltpu.VMEM((half, size), f32),
            pltpu.VMEM((half, size), f32),
            pltpu.VMEM((n, n * blocks, LANES), f32),
            dma((n,)), dma((n,)),
            dma((2, n)), dma((n,)),
            dma((2, n // 2)), dma((n // 2,)),
            dma((n // 2,)), dma((n // 2,)),
            dma((count, 2, n)), dma((count, n)),
            dma((count, 2, n)), dma((count, n)),
            dma((count, 2, n)), dma((count, n)),
            dma((count, 2, n)), dma((count, n)),
            dma((count,)), dma((count,)),
        ],
        compiler_params=pltpu.CompilerParams(
            collective_id=0, has_side_effects=True, vmem_limit_bytes=56 * 2**20
        ),
        cost_estimate=pl.CostEstimate(
            flops=4 * n * half * size * size, bytes_accessed=4 * size * size, transcendentals=0
        ),
    )(density, density_mask, square_mask, result_mask, block_perm)


def solution(mesh):
    in_specs = (P("row", "col"), P("row", "col"), P("row", "col"), P("row", "col"), P())
    return jax.shard_map(
        functools.partial(per_device, mesh.shape["row"], mesh.shape["layer"]),
        mesh=mesh,
        in_specs=in_specs,
        out_specs=P("row", "col"),
        check_vma=False,
    )
```

```python
import functools

import jax
import jax.numpy as jnp
from jax import lax
from jax.experimental import pallas as pl
from jax.experimental.pallas import tpu as pltpu
from jax.sharding import PartitionSpec as P

MESH = pl.DeviceIdType.MESH
LANES = 128


CHUNKS = 3


def row_chunks(rows):
    groups = rows // 16
    sizes = [16 * (groups // CHUNKS + (j < groups % CHUNKS)) for j in range(CHUNKS)]
    return tuple((sum(sizes[:j]), sizes[j]) for j in range(CHUNKS))


def tail_groups(rows, tail):
    per = LANES // tail
    high = -(-rows // (16 * per)) * 16
    assert rows % high == 0
    return high, rows // high


def copy_to(src, dst, send_sem, recv_sem, device):
    return pltpu.make_async_remote_copy(
        src_ref=src,
        dst_ref=dst,
        send_sem=send_sem,
        recv_sem=recv_sem,
        device_id=device,
        device_id_type=MESH,
    )


class Line:
    def __init__(self, part, send, recv, pos, count, device):
        self.part, self.send, self.recv = part, send, recv
        self.pos, self.count, self.device = pos, count, device

    def copy(self, k, way):
        part = self.part(k)
        target = self.device(self.pos + (1, -1)[way])
        return copy_to(part, part, self.send.at[way, k], self.recv.at[k], target)

    def has(self, way):
        return (self.pos < self.count - 1, self.pos > 0)[way]

    def start(self, k, way):
        @pl.when(self.has(way))
        def _():
            self.copy(k, way).start()

    def start_own(self):
        self.start(self.pos, 0)
        self.start(self.pos, 1)

    def step(self, s, then=None):
        for way in (0, 1):
            k = self.pos + (-s, s)[way]

            @pl.when(jnp.logical_and(k >= 0, k < self.count))
            def _():
                self.copy(k, 1 - way).wait_recv()
                self.start(k, way)
                if then is not None:
                    then(k)

    def wait_sends(self):
        for k in range(self.count):
            for way in (0, 1):
                held = (k <= self.pos, k >= self.pos)[way]

                @pl.when(jnp.logical_and(held, self.has(way)))
                def _():
                    self.copy(k, way).wait_send()


def spread(size, width, blocks, along):
    shape = (size, blocks) if along == 0 else (blocks, size)
    element = lax.broadcasted_iota(jnp.int32, shape, along)
    block = lax.broadcasted_iota(jnp.int32, shape, 1 - along)
    inside = jnp.logical_and(element >= block * width, element < (block + 1) * width)
    return inside.astype(jnp.float32)


def dot(a, b):
    return jnp.dot(a, b, preferred_element_type=jnp.float32)


def shift(tail, g, wide):
    shape = (tail, LANES) if wide else (LANES, tail)
    narrow = lax.broadcasted_iota(jnp.int32, shape, 1 - wide)
    lane = lax.broadcasted_iota(jnp.int32, shape, int(wide))
    return (lane == g * tail + narrow).astype(jnp.bfloat16)


def pack(src, k, off, rows, dst, j, main, tail):
    high, count = tail_groups(rows, tail)
    total = jnp.zeros((high, LANES), jnp.float32)
    for g in range(count):
        at = off + g * high
        total = total + dot(src[k, at:at + high, main:main + tail], shift(tail, g, True))
    dst[k, j, 0:high, :] = total.astype(jnp.bfloat16)


def unpack(src, k, j, off, rows, dst, main, tail):
    high, count = tail_groups(rows, tail)
    packed = src[k, j, 0:high, :]
    for g in range(count):
        at = off + g * high
        dst[k, at:at + high, main:main + tail] = dot(packed, shift(tail, g, False)).astype(jnp.bfloat16)


def kernel(n, layers, dens, dmask, smask, rmask, perm, out, B, A, S, AT, ST, acc, keep_s, keep_r, G,
           m_send, m_recv, g_send, g_recv, b_send, b_recv, t_send, t_recv,
           a_send, a_recv, s_send, s_recv, at_send, at_recv, st_send, st_recv, x_send, x_recv):
    l = lax.axis_index("layer")
    r = lax.axis_index("row")
    c = lax.axis_index("col")
    size = dens.shape[0]
    blocks = dmask.shape[0]
    width = size // blocks
    half = size // layers
    half_blocks = blocks // layers
    chunks = row_chunks(half)
    tail = size % LANES
    main = size - tail
    y, core = r // 2, r % 2
    ny = n // 2
    twin = {"row": y * 2 + 1 - core}
    other = {"layer": 1 - l}

    barrier = pltpu.get_barrier_semaphore()
    for step in range(1, n):
        pl.semaphore_signal(barrier, 1, device_id={"row": (r + step) % n}, device_id_type=MESH)
    pl.semaphore_signal(barrier, 1, device_id=other, device_id_type=MESH)

    @pl.when(c > 0)
    def _():
        pl.semaphore_signal(barrier, 1, device_id={"col": c - 1}, device_id_type=MESH)

    @pl.when(c < n - 1)
    def _():
        pl.semaphore_signal(barrier, 1, device_id={"col": c + 1}, device_id_type=MESH)

    lane = lax.broadcasted_iota(jnp.int32, (blocks, LANES), 1)
    line_no = lax.broadcasted_iota(jnp.int32, (blocks, LANES), 0)
    put_s = (lane == c * blocks + line_no).astype(jnp.float32)
    put_r = (lane == LANES // 2 + c * blocks + line_no).astype(jnp.float32)
    mine = pl.ds(pl.multiple_of(r * blocks, 8), blocks)
    G[c, mine, :] = dot(smask[...].astype(jnp.float32), put_s) + dot(rmask[...].astype(jnp.float32), put_r)

    rows_of = dot(spread(size, width, blocks, 0), dmask[...].astype(jnp.float32))
    keep = dot(rows_of, spread(size, width, blocks, 1))
    masked = jnp.where(keep > 0.5, dens[...], jnp.zeros_like(dens[...]))
    B[r] = masked
    top = pl.ds(pl.multiple_of(l * half, 16), half)
    A[c] = B[r, top, :]
    for j, (off, rows) in enumerate(chunks):
        pack(A, c, off, rows, AT, j, main, tail)

    ends = jnp.where(c == 0, 1, 0) + jnp.where(c == n - 1, 1, 0)
    pl.semaphore_wait(barrier, n + 2 - ends)

    def mask_copy(step):
        place = G.at[c, mine]
        return copy_to(place, place, m_send.at[step], m_recv.at[step], {"row": (r + step) % n})

    for step in range(1, n):
        mask_copy(step).start()

    def at_col(k):
        return {"col": k}

    def lines_of(whole_part, tail_part, send, recv, tail_send, tail_recv):
        made = []
        for j, (off, rows) in enumerate(chunks):
            high, _ = tail_groups(rows, tail)
            made.append((
                Line(lambda k, j=j, high=high: tail_part.at[k, j, pl.ds(0, high)],
                     tail_send.at[j], tail_recv.at[j], c, n, at_col),
                Line(lambda k, off=off, rows=rows: whole_part.at[k, pl.ds(off, rows), pl.ds(0, main)],
                     send.at[j], recv.at[j], c, n, at_col),
            ))
        return made

    a_lines = lines_of(A, AT, a_send, a_recv, at_send, at_recv)
    s_lines = lines_of(S, ST, s_send, s_recv, st_send, st_recv)

    def start_own(pair):
        for line in pair:
            line.start_own()

    def step_all(pair, s):
        for line in pair:
            line.step(s)

    g_line = Line(lambda k: G.at[k], g_send, g_recv, c, n, at_col)
    b_line = Line(lambda k: B.at[k * 2 + core], b_send, b_recv, y, ny, lambda k: {"row": k * 2 + core})

    def twin_copy(k):
        place = B.at[k * 2 + core]
        return copy_to(place, place, t_send.at[k], t_recv.at[k], twin)

    for pair in a_lines:
        start_own(pair)
    b_line.start_own()
    twin_copy(y).start()

    for step in range(1, n):
        mask_copy(step).wait_recv()
    g_line.start_own()
    for pair in a_lines:
        step_all(pair, 1)
    g_line.step(1)
    for s in range(2, n):
        g_line.step(s)
        for pair in a_lines if s < n - 1 else ():
            step_all(pair, s)
        if s - 1 < ny:
            b_line.step(s - 1, lambda k: twin_copy(k).start())
    for k in range(ny):
        place = B.at[k * 2 + 1 - core]
        copy_to(place, place, t_send.at[k], t_recv.at[k], twin).wait_recv()

    whole = G[0]
    for k in range(1, n):
        whole = whole + G[k]
    row_at = lax.broadcasted_iota(jnp.int32, (half, n * blocks), 0)
    row_to = jnp.zeros((half, n * blocks), jnp.int32)
    for t in range(half_blocks):
        row_to = jnp.where(row_at >= t * width, perm[r * blocks + l * half_blocks + t], row_to)
    pick_rows = (row_to == lax.broadcasted_iota(jnp.int32, (half, n * blocks), 1)).astype(jnp.float32)
    picked = dot(pick_rows, whole)
    col_at = lax.broadcasted_iota(jnp.int32, (LANES, size), 1)
    col_to = jnp.zeros((LANES, size), jnp.int32)
    for t in range(blocks):
        col_to = jnp.where(col_at >= t * width, perm[c * blocks + t], col_to)
    slot = lax.broadcasted_iota(jnp.int32, (LANES, size), 0)
    keep_s[...] = dot(picked, (col_to == slot).astype(jnp.float32))
    keep_r[...] = dot(picked, (col_to + LANES // 2 == slot).astype(jnp.float32))

    def product(left, tails, j, off, rows):
        acc[0:rows, :] = jnp.zeros((rows, size), jnp.float32)

        def body(k, carry):
            @pl.when(k != c)
            def _():
                unpack(tails, k, j, off, rows, left, main, tail)

            acc[0:rows, :] += dot(left[k, off:off + rows, :], B[k])
            return carry

        lax.fori_loop(0, n, body, 0)

    for j, (off, rows) in enumerate(chunks):
        step_all(a_lines[j], n - 1)
        product(A, AT, j, off, rows)
        value = jnp.where(keep_s[off:off + rows, :] > 0.5, acc[0:rows, :], 0.0)
        S[c, off:off + rows, :] = value.astype(jnp.bfloat16)
        pack(S, c, off, rows, ST, j, main, tail)
        start_own(s_lines[j])

    def result_copy(j):
        off, rows = chunks[j]
        place = out.at[pl.ds(pl.multiple_of(l * half + off, 16), rows)]
        return copy_to(place, place, x_send.at[j], x_recv.at[j], other)

    for s in range(1, n - 1):
        for pair in s_lines:
            step_all(pair, s)
    for j, (off, rows) in enumerate(chunks):
        step_all(s_lines[j], n - 1)
        product(S, ST, j, off, rows)
        value = 3.0 * S[c, off:off + rows, :].astype(jnp.float32) - 2.0 * acc[0:rows, :]
        value = jnp.where(keep_r[off:off + rows, :] > 0.5, value, 0.0)
        out[pl.ds(pl.multiple_of(l * half + off, 16), rows), :] = value.astype(jnp.bfloat16)
        result_copy(j).start()

    for j, (off, rows) in enumerate(chunks):
        place = out.at[pl.ds(pl.multiple_of((1 - l) * half + off, 16), rows)]
        copy_to(place, place, x_send.at[j], x_recv.at[j], other).wait_recv()
        result_copy(j).wait_send()
    for line in (g_line, b_line, *(line for pair in (*a_lines, *s_lines) for line in pair)):
        line.wait_sends()
    for k in range(ny):
        twin_copy(k).wait_send()
    for step in range(1, n):
        mask_copy(step).wait_send()


def per_device(n, layers, density, density_mask, square_mask, result_mask, block_perm):
    size = density.shape[0]
    half = size // layers
    blocks = density_mask.shape[0]
    pieces = row_chunks(half)
    count = len(pieces)
    most = max(rows for _, rows in pieces)
    high = max(tail_groups(rows, size % LANES)[0] for _, rows in pieces)
    bf16, f32 = jnp.bfloat16, jnp.float32
    dma = pltpu.SemaphoreType.DMA
    vmem = pl.BlockSpec(memory_space=pltpu.VMEM)
    return pl.pallas_call(
        functools.partial(kernel, n, layers),
        out_shape=jax.ShapeDtypeStruct((size, size), bf16),
        in_specs=[vmem] * 4 + [pl.BlockSpec(memory_space=pltpu.SMEM)],
        out_specs=vmem,
        scratch_shapes=[
            pltpu.VMEM((n, size, size), bf16),
            pltpu.VMEM((n, half, size), bf16),
            pltpu.VMEM((n, half, size), bf16),
            pltpu.VMEM((n, count, high, LANES), bf16),
            pltpu.VMEM((n, count, high, LANES), bf16),
            pltpu.VMEM((most, size), f32),
            pltpu.VMEM((half, size), f32),
            pltpu.VMEM((half, size), f32),
            pltpu.VMEM((n, n * blocks, LANES), f32),
            dma((n,)), dma((n,)),
            dma((2, n)), dma((n,)),
            dma((2, n // 2)), dma((n // 2,)),
            dma((n // 2,)), dma((n // 2,)),
            dma((count, 2, n)), dma((count, n)),
            dma((count, 2, n)), dma((count, n)),
            dma((count, 2, n)), dma((count, n)),
            dma((count, 2, n)), dma((count, n)),
            dma((count,)), dma((count,)),
        ],
        compiler_params=pltpu.CompilerParams(
            collective_id=0, has_side_effects=True, vmem_limit_bytes=56 * 2**20
        ),
        cost_estimate=pl.CostEstimate(
            flops=4 * n * half * size * size, bytes_accessed=4 * size * size, transcendentals=0
        ),
    )(density, density_mask, square_mask, result_mask, block_perm)


def solution(mesh):
    in_specs = (P("row", "col"), P("row", "col"), P("row", "col"), P("row", "col"), P())
    return jax.shard_map(
        functools.partial(per_device, mesh.shape["row"], mesh.shape["layer"]),
        mesh=mesh,
        in_specs=in_specs,
        out_specs=P("row", "col"),
        check_vma=False,
    )
```

```python
import functools

import jax
import jax.numpy as jnp
from jax import lax
from jax.experimental import pallas as pl
from jax.experimental.pallas import tpu as pltpu
from jax.sharding import PartitionSpec as P

MESH = pl.DeviceIdType.MESH
LANES = 128


CHUNKS = 5


def row_chunks(rows):
    sizes = [rows - 64 * (CHUNKS - 1)] + [64] * (CHUNKS - 1)
    return tuple((sum(sizes[:j]), sizes[j]) for j in range(CHUNKS))


def tail_groups(rows, tail):
    per = LANES // tail
    high = -(-rows // (16 * per)) * 16
    assert rows % high == 0
    return high, rows // high


def copy_to(src, dst, send_sem, recv_sem, device):
    return pltpu.make_async_remote_copy(
        src_ref=src,
        dst_ref=dst,
        send_sem=send_sem,
        recv_sem=recv_sem,
        device_id=device,
        device_id_type=MESH,
    )


class Line:
    def __init__(self, part, send, recv, pos, count, device):
        self.part, self.send, self.recv = part, send, recv
        self.pos, self.count, self.device = pos, count, device

    def copy(self, k, way):
        part = self.part(k)
        target = self.device(self.pos + (1, -1)[way])
        return copy_to(part, part, self.send.at[way, k], self.recv.at[k], target)

    def has(self, way):
        return (self.pos < self.count - 1, self.pos > 0)[way]

    def start(self, k, way):
        @pl.when(self.has(way))
        def _():
            self.copy(k, way).start()

    def start_own(self):
        self.start(self.pos, 0)
        self.start(self.pos, 1)

    def step(self, s, then=None):
        for way in (0, 1):
            k = self.pos + (-s, s)[way]

            @pl.when(jnp.logical_and(k >= 0, k < self.count))
            def _():
                self.copy(k, 1 - way).wait_recv()
                self.start(k, way)
                if then is not None:
                    then(k)

    def wait_sends(self):
        for k in range(self.count):
            for way in (0, 1):
                held = (k <= self.pos, k >= self.pos)[way]

                @pl.when(jnp.logical_and(held, self.has(way)))
                def _():
                    self.copy(k, way).wait_send()


def spread(size, width, blocks, along):
    shape = (size, blocks) if along == 0 else (blocks, size)
    element = lax.broadcasted_iota(jnp.int32, shape, along)
    block = lax.broadcasted_iota(jnp.int32, shape, 1 - along)
    inside = jnp.logical_and(element >= block * width, element < (block + 1) * width)
    return inside.astype(jnp.float32)


def dot(a, b):
    return jnp.dot(a, b, preferred_element_type=jnp.float32)


def shift(tail, g, wide):
    shape = (tail, LANES) if wide else (LANES, tail)
    narrow = lax.broadcasted_iota(jnp.int32, shape, 1 - wide)
    lane = lax.broadcasted_iota(jnp.int32, shape, int(wide))
    return (lane == g * tail + narrow).astype(jnp.bfloat16)


def pack(src, k, off, rows, dst, j, main, tail):
    high, count = tail_groups(rows, tail)
    total = jnp.zeros((high, LANES), jnp.float32)
    for g in range(count):
        at = off + g * high
        total = total + dot(src[k, at:at + high, main:main + tail], shift(tail, g, True))
    dst[k, j, 0:high, :] = total.astype(jnp.bfloat16)


def unpack(src, k, j, off, rows, dst, main, tail):
    high, count = tail_groups(rows, tail)
    packed = src[k, j, 0:high, :]
    for g in range(count):
        at = off + g * high
        dst[k, at:at + high, main:main + tail] = dot(packed, shift(tail, g, False)).astype(jnp.bfloat16)


def kernel(n, layers, dens, dmask, smask, rmask, perm, out, B, A, S, AT, ST, acc, keep_s, keep_r, G,
           m_send, m_recv, g_send, g_recv, b_send, b_recv, t_send, t_recv,
           a_send, a_recv, s_send, s_recv, at_send, at_recv, st_send, st_recv, x_send, x_recv):
    l = lax.axis_index("layer")
    r = lax.axis_index("row")
    c = lax.axis_index("col")
    size = dens.shape[0]
    blocks = dmask.shape[0]
    width = size // blocks
    half = size // layers
    half_blocks = blocks // layers
    chunks = row_chunks(half)
    tail = size % LANES
    main = size - tail
    y, core = r // 2, r % 2
    ny = n // 2
    twin = {"row": y * 2 + 1 - core}
    other = {"layer": 1 - l}

    barrier = pltpu.get_barrier_semaphore()
    for step in range(1, n):
        pl.semaphore_signal(barrier, 1, device_id={"row": (r + step) % n}, device_id_type=MESH)
    pl.semaphore_signal(barrier, 1, device_id=other, device_id_type=MESH)

    @pl.when(c > 0)
    def _():
        pl.semaphore_signal(barrier, 1, device_id={"col": c - 1}, device_id_type=MESH)

    @pl.when(c < n - 1)
    def _():
        pl.semaphore_signal(barrier, 1, device_id={"col": c + 1}, device_id_type=MESH)

    lane = lax.broadcasted_iota(jnp.int32, (blocks, LANES), 1)
    line_no = lax.broadcasted_iota(jnp.int32, (blocks, LANES), 0)
    put_s = (lane == c * blocks + line_no).astype(jnp.float32)
    put_r = (lane == LANES // 2 + c * blocks + line_no).astype(jnp.float32)
    mine = pl.ds(pl.multiple_of(r * blocks, 8), blocks)
    G[c, mine, :] = dot(smask[...].astype(jnp.float32), put_s) + dot(rmask[...].astype(jnp.float32), put_r)

    rows_of = dot(spread(size, width, blocks, 0), dmask[...].astype(jnp.float32))
    keep = dot(rows_of, spread(size, width, blocks, 1))
    masked = jnp.where(keep > 0.5, dens[...], jnp.zeros_like(dens[...]))
    B[r] = masked
    top = pl.ds(pl.multiple_of(l * half, 16), half)
    A[c] = B[r, top, :]
    for j, (off, rows) in enumerate(chunks):
        pack(A, c, off, rows, AT, j, main, tail)

    ends = jnp.where(c == 0, 1, 0) + jnp.where(c == n - 1, 1, 0)
    pl.semaphore_wait(barrier, n + 2 - ends)

    def mask_copy(step):
        place = G.at[c, mine]
        return copy_to(place, place, m_send.at[step], m_recv.at[step], {"row": (r + step) % n})

    for step in range(1, n):
        mask_copy(step).start()

    def at_col(k):
        return {"col": k}

    def lines_of(whole_part, tail_part, send, recv, tail_send, tail_recv):
        made = []
        for j, (off, rows) in enumerate(chunks):
            high, _ = tail_groups(rows, tail)
            made.append((
                Line(lambda k, j=j, high=high: tail_part.at[k, j, pl.ds(0, high)],
                     tail_send.at[j], tail_recv.at[j], c, n, at_col),
                Line(lambda k, off=off, rows=rows: whole_part.at[k, pl.ds(off, rows), pl.ds(0, main)],
                     send.at[j], recv.at[j], c, n, at_col),
            ))
        return made

    a_lines = lines_of(A, AT, a_send, a_recv, at_send, at_recv)
    s_lines = lines_of(S, ST, s_send, s_recv, st_send, st_recv)

    def start_own(pair):
        for line in pair:
            line.start_own()

    def step_all(pair, s):
        for line in pair:
            line.step(s)

    g_line = Line(lambda k: G.at[k], g_send, g_recv, c, n, at_col)
    b_line = Line(lambda k: B.at[k * 2 + core], b_send, b_recv, y, ny, lambda k: {"row": k * 2 + core})

    def twin_copy(k):
        place = B.at[k * 2 + core]
        return copy_to(place, place, t_send.at[k], t_recv.at[k], twin)

    for pair in a_lines:
        start_own(pair)
    b_line.start_own()
    twin_copy(y).start()

    for step in range(1, n):
        mask_copy(step).wait_recv()
    g_line.start_own()
    for pair in a_lines:
        step_all(pair, 1)
    g_line.step(1)
    for s in range(2, n):
        g_line.step(s)
        for pair in a_lines if s < n - 1 else ():
            step_all(pair, s)
        if s - 1 < ny:
            b_line.step(s - 1, lambda k: twin_copy(k).start())
    for k in range(ny):
        place = B.at[k * 2 + 1 - core]
        copy_to(place, place, t_send.at[k], t_recv.at[k], twin).wait_recv()

    whole = G[0]
    for k in range(1, n):
        whole = whole + G[k]
    row_at = lax.broadcasted_iota(jnp.int32, (half, n * blocks), 0)
    row_to = jnp.zeros((half, n * blocks), jnp.int32)
    for t in range(half_blocks):
        row_to = jnp.where(row_at >= t * width, perm[r * blocks + l * half_blocks + t], row_to)
    pick_rows = (row_to == lax.broadcasted_iota(jnp.int32, (half, n * blocks), 1)).astype(jnp.float32)
    picked = dot(pick_rows, whole)
    col_at = lax.broadcasted_iota(jnp.int32, (LANES, size), 1)
    col_to = jnp.zeros((LANES, size), jnp.int32)
    for t in range(blocks):
        col_to = jnp.where(col_at >= t * width, perm[c * blocks + t], col_to)
    slot = lax.broadcasted_iota(jnp.int32, (LANES, size), 0)
    keep_s[...] = dot(picked, (col_to == slot).astype(jnp.float32))
    keep_r[...] = dot(picked, (col_to + LANES // 2 == slot).astype(jnp.float32))

    def product(left, tails, j, off, rows):
        acc[0:rows, :] = jnp.zeros((rows, size), jnp.float32)

        def body(k, carry):
            @pl.when(k != c)
            def _():
                unpack(tails, k, j, off, rows, left, main, tail)

            acc[0:rows, :] += dot(left[k, off:off + rows, :], B[k])
            return carry

        lax.fori_loop(0, n, body, 0)

    for j, (off, rows) in enumerate(chunks):
        step_all(a_lines[j], n - 1)
        product(A, AT, j, off, rows)
        value = jnp.where(keep_s[off:off + rows, :] > 0.5, acc[0:rows, :], 0.0)
        S[c, off:off + rows, :] = value.astype(jnp.bfloat16)
        pack(S, c, off, rows, ST, j, main, tail)
        start_own(s_lines[j])

    def result_copy(j):
        off, rows = chunks[j]
        place = out.at[pl.ds(pl.multiple_of(l * half + off, 16), rows)]
        return copy_to(place, place, x_send.at[j], x_recv.at[j], other)

    for s in range(1, n - 1):
        for pair in s_lines:
            step_all(pair, s)
    for j, (off, rows) in enumerate(chunks):
        step_all(s_lines[j], n - 1)
        product(S, ST, j, off, rows)
        value = 3.0 * S[c, off:off + rows, :].astype(jnp.float32) - 2.0 * acc[0:rows, :]
        value = jnp.where(keep_r[off:off + rows, :] > 0.5, value, 0.0)
        out[pl.ds(pl.multiple_of(l * half + off, 16), rows), :] = value.astype(jnp.bfloat16)
        result_copy(j).start()

    for j, (off, rows) in enumerate(chunks):
        place = out.at[pl.ds(pl.multiple_of((1 - l) * half + off, 16), rows)]
        copy_to(place, place, x_send.at[j], x_recv.at[j], other).wait_recv()
        result_copy(j).wait_send()
    for line in (g_line, b_line, *(line for pair in (*a_lines, *s_lines) for line in pair)):
        line.wait_sends()
    for k in range(ny):
        twin_copy(k).wait_send()
    for step in range(1, n):
        mask_copy(step).wait_send()


def per_device(n, layers, density, density_mask, square_mask, result_mask, block_perm):
    size = density.shape[0]
    half = size // layers
    blocks = density_mask.shape[0]
    pieces = row_chunks(half)
    count = len(pieces)
    most = max(rows for _, rows in pieces)
    high = max(tail_groups(rows, size % LANES)[0] for _, rows in pieces)
    bf16, f32 = jnp.bfloat16, jnp.float32
    dma = pltpu.SemaphoreType.DMA
    vmem = pl.BlockSpec(memory_space=pltpu.VMEM)
    return pl.pallas_call(
        functools.partial(kernel, n, layers),
        out_shape=jax.ShapeDtypeStruct((size, size), bf16),
        in_specs=[vmem] * 4 + [pl.BlockSpec(memory_space=pltpu.SMEM)],
        out_specs=vmem,
        scratch_shapes=[
            pltpu.VMEM((n, size, size), bf16),
            pltpu.VMEM((n, half, size), bf16),
            pltpu.VMEM((n, half, size), bf16),
            pltpu.VMEM((n, count, high, LANES), bf16),
            pltpu.VMEM((n, count, high, LANES), bf16),
            pltpu.VMEM((most, size), f32),
            pltpu.VMEM((half, size), f32),
            pltpu.VMEM((half, size), f32),
            pltpu.VMEM((n, n * blocks, LANES), f32),
            dma((n,)), dma((n,)),
            dma((2, n)), dma((n,)),
            dma((2, n // 2)), dma((n // 2,)),
            dma((n // 2,)), dma((n // 2,)),
            dma((count, 2, n)), dma((count, n)),
            dma((count, 2, n)), dma((count, n)),
            dma((count, 2, n)), dma((count, n)),
            dma((count, 2, n)), dma((count, n)),
            dma((count,)), dma((count,)),
        ],
        compiler_params=pltpu.CompilerParams(
            collective_id=0, has_side_effects=True, vmem_limit_bytes=56 * 2**20
        ),
        cost_estimate=pl.CostEstimate(
            flops=4 * n * half * size * size, bytes_accessed=4 * size * size, transcendentals=0
        ),
    )(density, density_mask, square_mask, result_mask, block_perm)


def solution(mesh):
    in_specs = (P("row", "col"), P("row", "col"), P("row", "col"), P("row", "col"), P())
    return jax.shard_map(
        functools.partial(per_device, mesh.shape["row"], mesh.shape["layer"]),
        mesh=mesh,
        in_specs=in_specs,
        out_specs=P("row", "col"),
        check_vma=False,
    )
```
